32 devices in a mesh: layer: 8 (over y, x, core), tile: 4 (over z).
Axes of the slice: x: 2, y: 2, z: 4, core: 2. Of those that a mesh axis runs over, the one named last changes fastest.
Arguments:
- down_tiles: bfloat16 [8, 16, 3, 2, 512, 512], P('layer', 'tile'), may hold values from -0.109375 to 0.109375
- up_tiles: bfloat16 [8, 16, 3, 2, 512, 512], P('layer', 'tile'), may hold values from -0.109375 to 0.109375
- down_source: float32 [8, 2, 32, 8192], P('layer', None, None, 'tile'), may hold values from -3 to 3
- up_source: float32 [8, 2, 32, 8192], P('layer', None, None, 'tile'), may hold values from -3 to 3
- thickness: int32 [8], P('layer'), may hold values from 1 to 2
Outputs:
- field: float32 [8, 2, 32, 8192], P('layer', None, None, 'tile')
The draws below stay inside these ranges and needn't reach their ends.
All inputs are finite; a program needn't handle non-finite values.
Results may differ from the reference program's by a relative error of at most 0.04.
Values may be sent and summed in bfloat16 or wider, within the bound.
A program may use at most 128 MiB of HBM per device.

```python
import jax
import jax.numpy as jnp
from jax import lax

TILE = 512
PTS = 8192
LAYERS = 8
BLOCKS = 16
ALLCOLS = 32


def with_ends(values, stream_key, smallest, largest):
    index_at = [jax.random.randint(jax.random.fold_in(stream_key, axis), (), 0, length) for axis, length in enumerate(values.shape)]
    main_axis = values.shape.index(max(values.shape))
    neighbour = index_at[:main_axis] + [(index_at[main_axis] + 1) % values.shape[main_axis]] + index_at[main_axis + 1:]
    return values.at[tuple(index_at)].set(smallest).at[tuple(neighbour)].set(largest)


def shard_levels(own_key, dims, split, least, top_value):
    def one(axis_at, parts):
        draws = jax.random.uniform(jax.random.fold_in(jax.random.fold_in(own_key, 6), axis_at), (parts,), jnp.float32, least / len(split), top_value / len(split))
        return jnp.repeat(jnp.exp(draws), dims[axis_at] // parts).reshape((-1,) + (1,) * (len(dims) - axis_at - 1))

    factor_of = one(*split[0])
    for cut in split[1:]:
        factor_of = factor_of * one(*cut)
    return factor_of


def normal_values(own_key, extent, deviation, reach, pieces=(), held_as=jnp.bfloat16):
    drawn = deviation * jax.random.normal(own_key, extent, jnp.float32)
    if pieces:
        drawn = drawn * shard_levels(own_key, extent, pieces, -0.22, 0.18)
    return jnp.clip(drawn, -reach, reach).astype(held_as)


def setup_inputs(seed: int = 0) -> dict:
    streams_of = jax.random.split(jax.random.key(seed), 6)
    return {
        "down_tiles": normal_values(streams_of[0], (LAYERS, BLOCKS, 3, 2, TILE, TILE), (6 * TILE) ** -0.5, 0.109375, ((0, 8), (1, 4))),
        "up_tiles": normal_values(streams_of[1], (LAYERS, BLOCKS, 3, 2, TILE, TILE), (6 * TILE) ** -0.5, 0.109375, ((0, 8), (1, 4))),
        "down_source": normal_values(streams_of[2], (LAYERS, 2, ALLCOLS, PTS), 0.5, 3.0, ((0, 8), (3, 4)), jnp.float32),
        "up_source": normal_values(streams_of[3], (LAYERS, 2, ALLCOLS, PTS), 0.5, 3.0, ((0, 8), (3, 4)), jnp.float32),
        "thickness": with_ends(jax.random.randint(streams_of[4], (LAYERS,), 1, 3), jax.random.fold_in(streams_of[4], 1), 1, 2).astype(jnp.int32),
    }


def apply_layer(layer_tiles, trace_in):
    columns = trace_in.shape[1]
    trace_in = lax.optimization_barrier(trace_in)
    blocks = trace_in.reshape(2, columns, BLOCKS, TILE).astype(jnp.float32)
    padded = jnp.pad(blocks, ((0, 0), (0, 0), (1, 1), (0, 0)))
    accum = jnp.zeros((2, 2, columns, BLOCKS, TILE), jnp.float32)
    for offset in range(3):
        window = padded[:, :, offset:offset + BLOCKS, :]
        accum = accum + jnp.einsum("pcbt,bqtu->pqcbu", window, layer_tiles[:, offset].astype(jnp.float32))
    real_part = accum[0, 0] - accum[1, 1]
    imag_part = accum[0, 1] + accum[1, 0]
    return jnp.stack([real_part, imag_part]).reshape(2, columns, PTS)


def transfer(layer_tiles, state_in, layer_thick):
    first_power = apply_layer(layer_tiles, state_in.astype(jnp.bfloat16))
    return lax.cond(layer_thick == 2,
                    lambda: apply_layer(layer_tiles, first_power.astype(jnp.bfloat16)),
                    lambda: first_power)


def sweep_step(state_in, layer_item):
    layer_tiles, source, layer_thick = layer_item
    updated = source + transfer(layer_tiles, state_in, layer_thick)
    return updated, updated


def reference(down_tiles, up_tiles, down_source, up_source, thickness):
    zeros_init = jnp.zeros((2, ALLCOLS, PTS), jnp.float32)
    _, downward = lax.scan(sweep_step, zeros_init, (down_tiles, down_source, thickness))
    _, upward = lax.scan(sweep_step, zeros_init, (up_tiles, up_source, thickness), reverse=True)
    return downward + upward
```

```python
import functools

import jax
import jax.numpy as jnp
from jax import lax
from jax.experimental import pallas as pl
from jax.experimental.pallas import tpu as pltpu
from jax.sharding import PartitionSpec as P

MESH = pl.DeviceIdType.MESH


def sweep_kernel(
    layers, tiles, rows, width, cols,
    down_tiles, up_tiles, down_source, up_source, thick_ref, out_ref,
    weights, source, inbox, wide, accum, first, outbox,
    tile_sem, source_sem, recv_sem, next_sem, rim_sem, mid_sem,
):
    layer = lax.axis_index("layer")
    tile = lax.axis_index("tile")
    height = 2 * cols
    depth = 2 * width
    slots = rows + 2
    has_low, has_high = tile > 0, tile < tiles - 1
    own_first = jnp.where(2 * layer < layers, 0, 1)

    groups = [g for g in (list(range(2, rows)), sorted({1, rows}), [0, rows + 1]) if g]

    def tile_copy(ref, direction, b, k):
        return pltpu.make_async_copy(
            ref.at[b, pl.ds(k * depth, depth)],
            weights.at[direction, b, pl.ds(k * depth, depth)],
            tile_sem.at[direction, b, k],
        )

    def source_copy(ref, direction, b):
        return pltpu.make_async_copy(
            ref.at[:, pl.ds(b * width, width)], source.at[direction, b], source_sem.at[direction, b]
        )

    tile_order = [(b, j - b) for g in groups for j in g for b in range(rows) if 0 <= j - b <= 2]

    def start_loads(ref, direction):
        for b, k in tile_order:
            tile_copy(ref, direction, b, k).start()

    for direction, ref in enumerate((down_source, up_source)):
        for b in range(rows):
            source_copy(ref, direction, b).start()

    @pl.when(own_first == 0)
    def _():
        start_loads(down_tiles, 0)
        start_loads(up_tiles, 1)

    @pl.when(own_first == 1)
    def _():
        start_loads(up_tiles, 1)
        start_loads(down_tiles, 0)

    barrier = pltpu.get_barrier_semaphore()
    met = 0
    for dl in (-1, 0, 1):
        for dt in (-1, 0, 1):
            if dl == 0 and dt == 0:
                continue
            there = (layer + dl >= 0) & (layer + dl < layers) & (tile + dt >= 0) & (tile + dt < tiles)

            @pl.when(there)
            def _(dl=dl, dt=dt):
                pl.semaphore_signal(
                    barrier, inc=1, device_id={"layer": layer + dl, "tile": tile + dt}, device_id_type=MESH
                )

            met = met + jnp.where(there, 1, 0)

    out_ref[...] = jnp.zeros_like(out_ref)
    no_trace = jnp.zeros((height, width), jnp.bfloat16)

    @pl.when(jnp.logical_not(has_low))
    def _():
        for direction in range(2):
            for phase in range(2):
                inbox[direction, phase, 0] = no_trace

    @pl.when(jnp.logical_not(has_high))
    def _():
        for direction in range(2):
            for phase in range(2):
                inbox[direction, phase, rows + 1] = no_trace

    pl.semaphore_wait(barrier, met)
    is_thick = jnp.full((height, width), thick_ref[0], jnp.int32) == 2

    def remote(src, direction, phase, slot, send_sem, to_layer, to_tile):
        return pltpu.make_async_remote_copy(
            src_ref=src,
            dst_ref=inbox.at[direction, phase, slot],
            send_sem=send_sem,
            recv_sem=recv_sem.at[direction, phase, slot],
            device_id={"layer": to_layer, "tile": to_tile},
            device_id_type=MESH,
        )

    def onward(direction, b):
        to_layer = layer + 1 - 2 * direction
        box = outbox.at[direction, b]
        copies = []
        if b == 0:
            copies.append((has_low, remote(
                box, direction, 0, rows + 1, rim_sem.at[direction, 0], to_layer, tile - 1)))
        if b == rows - 1:
            copies.append((has_high, remote(
                box, direction, 0, 0, rim_sem.at[direction, 1], to_layer, tile + 1)))
        copies.append((None, remote(
            box, direction, 0, b + 1, next_sem.at[direction, b], to_layer, tile)))
        return copies

    def sideways(direction, b):
        box = inbox.at[direction, 1, b + 1]
        copies = []
        if b == 0:
            copies.append((has_low, remote(
                box, direction, 1, rows + 1, mid_sem.at[direction, 0], layer, tile - 1)))
        if b == rows - 1:
            copies.append((has_high, remote(
                box, direction, 1, 0, mid_sem.at[direction, 1], layer, tile + 1)))
        return copies

    def each(copies, what):
        for condition, copy in copies:
            if condition is None:
                what(copy)
            else:
                pl.when(condition)(functools.partial(what, copy))

    def start(copy):
        copy.start()

    def sent(copy):
        copy.wait_send()

    def arrived(direction, phase, slot):
        def wait():
            remote(
                inbox.at[direction, phase, slot], direction, phase, slot,
                mid_sem.at[direction, 0], layer, tile,
            ).wait_recv()

        if slot == 0:
            pl.when(has_low)(wait)
        elif slot == rows + 1:
            pl.when(has_high)(wait)
        else:
            pl.when(phase == 0)(wait)

    def finish(direction, b, moved, has_next):
        columns = pl.ds(b * width, width)
        source_copy(down_source, direction, b).wait()
        value = source[direction, b]
        if moved is not None:
            value = value + moved
        out_ref[:, columns] += value

        @pl.when(has_next)
        def _():
            outbox[direction, b] = value.astype(jnp.bfloat16)
            each(onward(direction, b), start)

    def one_phase(phase, direction, has_next):
        touched = set()
        done = 0
        for group in groups:
            for j in group:
                arrived(direction, phase, j)
                x = inbox[direction, phase, j]
                wide[:, pl.ds(j * depth, width)] = x
                wide[:, pl.ds(j * depth + width, width)] = jnp.concatenate([-x[cols:], x[:cols]], axis=0)
            outs = [b for b in range(rows) if any(0 <= j - b <= 2 for j in group)]
            ready = []
            for b in outs:
                taps = [j - b for j in group if 0 <= j - b <= 2]

                @pl.when(phase == 0)
                def _(b=b, taps=taps):
                    for k in taps:
                        tile_copy(down_tiles, direction, b, k).wait()

                runs = []
                for k in taps:
                    if runs and runs[-1][1] == k:
                        runs[-1][1] = k + 1
                    else:
                        runs.append([k, k + 1])
                total = None
                for low, high in runs:
                    part = jnp.dot(
                        wide[:, pl.ds((b + low) * depth, (high - low) * depth)],
                        weights[direction, b, pl.ds(low * depth, (high - low) * depth)],
                        preferred_element_type=jnp.float32,
                    )
                    total = part if total is None else total + part
                accum[b] = accum[b] + total if b in touched else total
                touched.add(b)
                done |= sum(1 << (3 * b + k) for k in taps)
                if (done >> (3 * b)) & 7 == 7:
                    ready.append(b)

                    @pl.when(phase == 0)
                    def _(b=b):
                        first[b] = accum[b]
                        inbox[direction, 1, b + 1] = accum[b].astype(jnp.bfloat16)
                        each(sideways(direction, b), start)

                    @pl.when(phase == 1)
                    def _(b=b):
                        finish(direction, b, jnp.where(is_thick, accum[b], first[b]), has_next)

    def one_direction(step, carry):
        direction = (own_first + step) % 2
        begins = jnp.where(direction == 0, layer == 0, layer == layers - 1)
        has_next = jnp.where(direction == 0, layer < layers - 1, layer > 0)

        @pl.when(begins)
        def _():
            for b in sorted(range(rows), key=lambda b: 0 < b < rows - 1):
                finish(direction, b, None, has_next)
            for b, k in tile_order:
                tile_copy(down_tiles, direction, b, k).wait()

        @pl.when(jnp.logical_not(begins))
        def _():
            def body(phase, inner):
                one_phase(phase, direction, has_next)
                return inner

            lax.fori_loop(0, 2, body, 0)
            for b in range(rows):
                each(sideways(direction, b), sent)

        return carry

    lax.fori_loop(0, 2, one_direction, 0)
    for direction in range(2):
        has_next = layer < layers - 1 if direction == 0 else layer > 0

        @pl.when(has_next)
        def _(direction=direction):
            for b in range(rows):
                each(onward(direction, b), sent)


def shards(layers, tiles, down_tiles, up_tiles, down_source, up_source, thickness):
    _, rows, taps, parts, width, _ = down_tiles.shape
    cols = down_source.shape[2]
    height, depth = parts * cols, parts * width
    points = rows * width
    flat_tiles = (rows, taps * depth, width)
    flat = (height, points)
    anywhere = pl.BlockSpec(memory_space=pl.ANY)
    field = pl.pallas_call(
        functools.partial(sweep_kernel, layers, tiles, rows, width, cols),
        out_shape=jax.ShapeDtypeStruct(flat, jnp.float32),
        in_specs=[anywhere] * 4 + [pl.BlockSpec(memory_space=pltpu.SMEM)],
        out_specs=pl.BlockSpec(memory_space=pltpu.VMEM),
        scratch_shapes=[
            pltpu.VMEM((2,) + flat_tiles, jnp.bfloat16),
            pltpu.VMEM((2, rows, height, width), jnp.float32),
            pltpu.VMEM((2, 2, rows + 2, height, width), jnp.bfloat16),
            pltpu.VMEM((height, (rows + 2) * depth), jnp.bfloat16),
            pltpu.VMEM((rows, height, width), jnp.float32),
            pltpu.VMEM((rows, height, width), jnp.float32),
            pltpu.VMEM((2, rows, height, width), jnp.bfloat16),
            pltpu.SemaphoreType.DMA((2, rows, taps)),
            pltpu.SemaphoreType.DMA((2, rows)),
            pltpu.SemaphoreType.DMA((2, 2, rows + 2)),
            pltpu.SemaphoreType.DMA((2, rows)),
            pltpu.SemaphoreType.DMA((2, 2)),
            pltpu.SemaphoreType.DMA((2, 2)),
        ],
        compiler_params=pltpu.CompilerParams(
            collective_id=0, has_side_effects=True, vmem_limit_bytes=48 * 1024 * 1024
        ),
        cost_estimate=pl.CostEstimate(
            flops=8 * rows * taps * height * depth * width,
            bytes_accessed=4 * rows * taps * depth * width,
            transcendentals=0,
        ),
    )(
        down_tiles.reshape(flat_tiles),
        up_tiles.reshape(flat_tiles),
        down_source.reshape(flat),
        up_source.reshape(flat),
        thickness,
    )
    return field.reshape(down_source.shape)


def solution(mesh):
    return jax.shard_map(
        functools.partial(shards, mesh.shape["layer"], mesh.shape["tile"]),
        mesh=mesh,
        in_specs=(
            P("layer", "tile", None, None, None, None),
            P("layer", "tile", None, None, None, None),
            P("layer", None, None, "tile"),
            P("layer", None, None, "tile"),
            P("layer"),
        ),
        out_specs=P("layer", None, None, "tile"),
        check_vma=False,
    )
```

```python
import functools

import jax
import jax.numpy as jnp
from jax import lax
from jax.experimental import pallas as pl
from jax.experimental.pallas import tpu as pltpu
from jax.sharding import PartitionSpec as P

MESH = pl.DeviceIdType.MESH


def sweep_kernel(
    layers, tiles, rows, width, cols,
    down_tiles, up_tiles, down_source, up_source, thick_ref, out_ref,
    weights, source, inbox, wide, accum, outbox,
    tile_sem, source_sem, recv_sem, next_sem, rim_sem, mid_sem,
):
    layer = lax.axis_index("layer")
    tile = lax.axis_index("tile")
    height = 2 * cols
    depth = 2 * width
    slots = rows + 2
    has_low, has_high = tile > 0, tile < tiles - 1
    own_first = jnp.where(2 * layer < layers, 0, 1)

    groups = [g for g in (list(range(2, rows)), sorted({1, rows}), [0, rows + 1]) if g]

    def tile_copy(ref, direction, b, k):
        return pltpu.make_async_copy(
            ref.at[b, pl.ds(k * depth, depth)],
            weights.at[direction, b, pl.ds(k * depth, depth)],
            tile_sem.at[direction, b, k],
        )

    def source_copy(ref, direction, b):
        return pltpu.make_async_copy(
            ref.at[:, pl.ds(b * width, width)], source.at[direction, b], source_sem.at[direction, b]
        )

    tile_order = [(b, j - b) for g in groups for j in g for b in range(rows) if 0 <= j - b <= 2]

    def start_loads(ref, direction):
        for b, k in tile_order:
            tile_copy(ref, direction, b, k).start()

    for direction, ref in enumerate((down_source, up_source)):
        for b in range(rows):
            source_copy(ref, direction, b).start()

    @pl.when(own_first == 0)
    def _():
        start_loads(down_tiles, 0)
        start_loads(up_tiles, 1)

    @pl.when(own_first == 1)
    def _():
        start_loads(up_tiles, 1)
        start_loads(down_tiles, 0)

    barrier = pltpu.get_barrier_semaphore()
    met = 0
    for dl in (-1, 0, 1):
        for dt in (-1, 0, 1):
            if dl == 0 and dt == 0:
                continue
            there = (layer + dl >= 0) & (layer + dl < layers) & (tile + dt >= 0) & (tile + dt < tiles)

            @pl.when(there)
            def _(dl=dl, dt=dt):
                pl.semaphore_signal(
                    barrier, inc=1, device_id={"layer": layer + dl, "tile": tile + dt}, device_id_type=MESH
                )

            met = met + jnp.where(there, 1, 0)

    out_ref[...] = jnp.zeros_like(out_ref)
    no_trace = jnp.zeros((height, width), jnp.bfloat16)

    @pl.when(jnp.logical_not(has_low))
    def _():
        for direction in range(2):
            for phase in range(2):
                inbox[direction, phase, 0] = no_trace

    @pl.when(jnp.logical_not(has_high))
    def _():
        for direction in range(2):
            for phase in range(2):
                inbox[direction, phase, rows + 1] = no_trace

    pl.semaphore_wait(barrier, met)
    is_thick = jnp.full((height, width), thick_ref[0], jnp.int32) == 2

    def remote(src, direction, phase, slot, send_sem, to_layer, to_tile):
        return pltpu.make_async_remote_copy(
            src_ref=src,
            dst_ref=inbox.at[direction, phase, slot],
            send_sem=send_sem,
            recv_sem=recv_sem.at[direction, phase, slot],
            device_id={"layer": to_layer, "tile": to_tile},
            device_id_type=MESH,
        )

    def onward(direction, b):
        to_layer = layer + 1 - 2 * direction
        box = outbox.at[direction, b]
        copies = []
        if b == 0:
            copies.append((has_low, remote(
                box, direction, 0, rows + 1, rim_sem.at[direction, 0], to_layer, tile - 1)))
        if b == rows - 1:
            copies.append((has_high, remote(
                box, direction, 0, 0, rim_sem.at[direction, 1], to_layer, tile + 1)))
        copies.append((None, remote(
            box, direction, 0, b + 1, next_sem.at[direction, b], to_layer, tile)))
        return copies

    def sideways(direction, b):
        box = inbox.at[direction, 1, b + 1]
        copies = []
        if b == 0:
            copies.append((has_low, remote(
                box, direction, 1, rows + 1, mid_sem.at[direction, 0], layer, tile - 1)))
        if b == rows - 1:
            copies.append((has_high, remote(
                box, direction, 1, 0, mid_sem.at[direction, 1], layer, tile + 1)))
        return copies

    def each(copies, what):
        for condition, copy in copies:
            if condition is None:
                what(copy)
            else:
                pl.when(condition)(functools.partial(what, copy))

    def start(copy):
        copy.start()

    def sent(copy):
        copy.wait_send()

    def arrived(direction, phase, slot):
        def wait():
            remote(
                inbox.at[direction, phase, slot], direction, phase, slot,
                mid_sem.at[direction, 0], layer, tile,
            ).wait_recv()

        if slot == 0:
            pl.when(has_low)(wait)
        elif slot == rows + 1:
            pl.when(has_high)(wait)
        else:
            pl.when(phase == 0)(wait)

    def finish(direction, b, moved, has_next):
        columns = pl.ds(b * width, width)
        source_copy(down_source, direction, b).wait()
        value = source[direction, b]
        if moved is not None:
            value = value + moved
        out_ref[:, columns] += value

        @pl.when(has_next)
        def _():
            outbox[direction, b] = value.astype(jnp.bfloat16)
            each(onward(direction, b), start)

    def one_phase(phase, direction, has_next):
        touched = set()
        edges = [b for b in range(rows) if b in (0, rows - 1)]
        for position, group in enumerate(groups):
            taps_of = {b: [j - b for j in group if 0 <= j - b <= 2] for b in range(rows)}
            taps_of = {b: taps for b, taps in taps_of.items() if taps}

            @pl.when(phase == 0)
            def _(taps_of=taps_of):
                for b, taps in taps_of.items():
                    for k in taps:
                        tile_copy(down_tiles, direction, b, k).wait()

            for j in group:
                arrived(direction, phase, j)
            for j in group:
                x = inbox[direction, phase, j]
                wide[:, pl.ds(j * depth, width)] = x
                wide[:, pl.ds(j * depth + width, width)] = jnp.concatenate([-x[cols:], x[:cols]], axis=0)
            for b, taps in taps_of.items():
                runs = []
                for k in taps:
                    if runs and runs[-1][1] == k:
                        runs[-1][1] = k + 1
                    else:
                        runs.append([k, k + 1])
                total = accum[phase, b] if b in touched else None
                for low, high in runs:
                    part = jnp.dot(
                        wide[:, pl.ds((b + low) * depth, (high - low) * depth)],
                        weights[direction, b, pl.ds(low * depth, (high - low) * depth)],
                        preferred_element_type=jnp.float32,
                    )
                    total = part if total is None else total + part
                accum[phase, b] = total
                touched.add(b)
            last = position == len(groups) - 1
            if last:
                inner = [b for b in range(rows) if b not in edges]

                @pl.when(phase == 0)
                def _():
                    for b in edges + inner:
                        inbox[direction, 1, b + 1] = accum[0, b].astype(jnp.bfloat16)
                        each(sideways(direction, b), start)

            ready = edges if last else [b for b in range(1, rows - 1) if position == len(groups) - 2]
            if ready:

                @pl.when(phase == 1)
                def _(ready=ready):
                    for b in ready:
                        finish(direction, b, jnp.where(is_thick, accum[1, b], accum[0, b]), has_next)

    def one_direction(step, carry):
        direction = (own_first + step) % 2
        begins = jnp.where(direction == 0, layer == 0, layer == layers - 1)
        has_next = jnp.where(direction == 0, layer < layers - 1, layer > 0)

        @pl.when(begins)
        def _():
            for b in sorted(range(rows), key=lambda b: 0 < b < rows - 1):
                finish(direction, b, None, has_next)
            for b, k in tile_order:
                tile_copy(down_tiles, direction, b, k).wait()

        @pl.when(jnp.logical_not(begins))
        def _():
            def body(phase, inner):
                one_phase(phase, direction, has_next)
                return inner

            lax.fori_loop(0, 2, body, 0)
            for b in range(rows):
                each(sideways(direction, b), sent)

        return carry

    lax.fori_loop(0, 2, one_direction, 0)
    for direction in range(2):
        has_next = layer < layers - 1 if direction == 0 else layer > 0

        @pl.when(has_next)
        def _(direction=direction):
            for b in range(rows):
                each(onward(direction, b), sent)


def shards(layers, tiles, down_tiles, up_tiles, down_source, up_source, thickness):
    _, rows, taps, parts, width, _ = down_tiles.shape
    cols = down_source.shape[2]
    height, depth = parts * cols, parts * width
    points = rows * width
    flat_tiles = (rows, taps * depth, width)
    flat = (height, points)
    anywhere = pl.BlockSpec(memory_space=pl.ANY)
    field = pl.pallas_call(
        functools.partial(sweep_kernel, layers, tiles, rows, width, cols),
        out_shape=jax.ShapeDtypeStruct(flat, jnp.float32),
        in_specs=[anywhere] * 4 + [pl.BlockSpec(memory_space=pltpu.SMEM)],
        out_specs=pl.BlockSpec(memory_space=pltpu.VMEM),
        scratch_shapes=[
            pltpu.VMEM((2,) + flat_tiles, jnp.bfloat16),
            pltpu.VMEM((2, rows, height, width), jnp.float32),
            pltpu.VMEM((2, 2, rows + 2, height, width), jnp.bfloat16),
            pltpu.VMEM((height, (rows + 2) * depth), jnp.bfloat16),
            pltpu.VMEM((2, rows, height, width), jnp.float32),
            pltpu.VMEM((2, rows, height, width), jnp.bfloat16),
            pltpu.SemaphoreType.DMA((2, rows, taps)),
            pltpu.SemaphoreType.DMA((2, rows)),
            pltpu.SemaphoreType.DMA((2, 2, rows + 2)),
            pltpu.SemaphoreType.DMA((2, rows)),
            pltpu.SemaphoreType.DMA((2, 2)),
            pltpu.SemaphoreType.DMA((2, 2)),
        ],
        compiler_params=pltpu.CompilerParams(
            collective_id=0, has_side_effects=True, vmem_limit_bytes=60 * 1024 * 1024
        ),
        cost_estimate=pl.CostEstimate(
            flops=8 * rows * taps * height * depth * width,
            bytes_accessed=4 * rows * taps * depth * width,
            transcendentals=0,
        ),
    )(
        down_tiles.reshape(flat_tiles),
        up_tiles.reshape(flat_tiles),
        down_source.reshape(flat),
        up_source.reshape(flat),
        thickness,
    )
    return field.reshape(down_source.shape)


def solution(mesh):
    return jax.shard_map(
        functools.partial(shards, mesh.shape["layer"], mesh.shape["tile"]),
        mesh=mesh,
        in_specs=(
            P("layer", "tile", None, None, None, None),
            P("layer", "tile", None, None, None, None),
            P("layer", None, None, "tile"),
            P("layer", None, None, "tile"),
            P("layer"),
        ),
        out_specs=P("layer", None, None, "tile"),
        check_vma=False,
    )
```

```python
import functools

import jax
import jax.numpy as jnp
from jax import lax
from jax.experimental import pallas as pl
from jax.experimental.pallas import tpu as pltpu
from jax.sharding import PartitionSpec as P

MESH = pl.DeviceIdType.MESH
PHASES = 4


def sweep_kernel(
    layers, tiles, rows, width, cols,
    down_tiles, up_tiles, down_source, up_source, thick_ref, out_ref,
    weights, source, inbox, wide, accum, outbox, field, got, thick,
    tile_sem, tile_sent, source_sem, source_sent, recv_sem, next_sem, rim_sem, side_sem,
    field_sem, field_sent, thick_sem, thick_sent,
):
    layer = lax.axis_index("layer")
    tile = lax.axis_index("tile")
    pairs, strips = layers // 2, tiles * 2
    pair, core = layer // 2, layer % 2
    other = 1 - core
    strip = tile * 2 + core
    height = 2 * cols
    depth = 2 * width
    has_low, has_high = strip > 0, strip < strips - 1
    own_first = jnp.where(2 * pair < pairs, 0, 1)

    groups = [g for g in (list(range(2, rows)), sorted({1, rows}), [0, rows + 1]) if g]
    tile_order = [(b, j - b) for g in groups for j in g for b in range(rows) if 0 <= j - b <= 2]
    edges_first = sorted(range(rows), key=lambda b: 0 < b < rows - 1)

    def device(to_pair, to_strip):
        return {"layer": 2 * to_pair + to_strip % 2, "tile": to_strip // 2}

    partner = {"layer": 2 * pair + other, "tile": tile}

    def columns(part, b):
        return pl.ds(pl.multiple_of((part * rows + b) * width, width), width)

    def tile_here(ref, direction, par, b, k):
        taps = pl.ds(k * depth, depth)
        return pltpu.make_async_copy(
            ref.at[core * rows + b, taps], weights.at[direction, par, b, taps],
            tile_sem.at[direction, par, b, k],
        )

    def tile_there(ref, direction, par, b, k):
        taps = pl.ds(k * depth, depth)
        return pltpu.make_async_remote_copy(
            src_ref=ref.at[other * rows + b, taps], dst_ref=weights.at[direction, par, b, taps],
            send_sem=tile_sent.at[direction, b, k], recv_sem=tile_sem.at[direction, par, b, k],
            device_id=partner, device_id_type=MESH,
        )

    def source_here(ref, direction, par, b):
        return pltpu.make_async_copy(
            ref.at[:, columns(core, b)], source.at[direction, par, b], source_sem.at[direction, par, b]
        )

    def source_there(ref, direction, par, b):
        return pltpu.make_async_remote_copy(
            src_ref=ref.at[:, columns(other, b)], dst_ref=source.at[direction, par, b],
            send_sem=source_sent.at[direction, b], recv_sem=source_sem.at[direction, par, b],
            device_id=partner, device_id_type=MESH,
        )

    def thick_there(par):
        return pltpu.make_async_remote_copy(
            src_ref=thick.at[par], dst_ref=thick.at[par], send_sem=thick_sent, recv_sem=thick_sem,
            device_id=partner, device_id_type=MESH,
        )

    def field_there(par, b):
        return pltpu.make_async_remote_copy(
            src_ref=field.at[par, b], dst_ref=got.at[b], send_sem=field_sent.at[b],
            recv_sem=field_sem.at[b], device_id=partner, device_id_type=MESH,
        )

    tile_refs, source_refs = (down_tiles, up_tiles), (down_source, up_source)
    used = (layer > 0, layer < layers - 1)

    def tiles_in_order(what):
        for first in range(2):

            @pl.when(own_first == first)
            def _(first=first):
                for direction in (first, 1 - first):

                    @pl.when(used[direction])
                    def _(direction=direction):
                        for b, k in tile_order:
                            what(tile_refs[direction], direction, core, b, k)

    for direction in range(2):
        for b in range(rows):
            source_here(source_refs[direction], direction, core, b).start()
    tiles_in_order(lambda *at: tile_here(*at).start())

    barrier = pltpu.get_barrier_semaphore()
    met = 0
    for dp in (-1, 0, 1):
        for ds in (-1, 0, 1):
            if dp == 0 and ds == 0:
                continue
            there = (pair + dp >= 0) & (pair + dp < pairs) & (strip + ds >= 0) & (strip + ds < strips)

            @pl.when(there)
            def _(dp=dp, ds=ds):
                pl.semaphore_signal(
                    barrier, inc=1, device_id=device(pair + dp, strip + ds), device_id_type=MESH
                )

            met = met + jnp.where(there, 1, 0)

    field[...] = jnp.zeros_like(field)
    thick[core] = jnp.full((height, width), thick_ref[0], jnp.int32)
    no_trace = jnp.zeros((height, width), jnp.bfloat16)
    for absent, slot in ((jnp.logical_not(has_low), 0), (jnp.logical_not(has_high), rows + 1)):

        @pl.when(absent)
        def _(slot=slot):
            for direction in range(2):
                for phase in range(PHASES):
                    inbox[direction, phase, slot] = no_trace

    pl.semaphore_wait(barrier, met)
    for direction in range(2):
        for b in range(rows):
            source_there(source_refs[direction], direction, core, b).start()
    thick_there(core).start()
    tiles_in_order(lambda *at: tile_there(*at).start())

    def remote(src, direction, phase, slot, send_sem, to_pair, to_strip):
        return pltpu.make_async_remote_copy(
            src_ref=src, dst_ref=inbox.at[direction, phase, slot], send_sem=send_sem,
            recv_sem=recv_sem.at[direction, phase, slot],
            device_id=device(to_pair, to_strip), device_id_type=MESH,
        )

    def onward(direction, b):
        to_pair = pair + 1 - 2 * direction
        box = outbox.at[direction, b]
        copies = []
        if b == 0:
            copies.append((has_low, remote(
                box, direction, 0, rows + 1, rim_sem.at[direction, 0], to_pair, strip - 1)))
        if b == rows - 1:
            copies.append((has_high, remote(
                box, direction, 0, 0, rim_sem.at[direction, 1], to_pair, strip + 1)))
        copies.append((None, remote(
            box, direction, 0, b + 1, next_sem.at[direction, b], to_pair, strip)))
        return copies

    def sideways(direction, phase, b):
        box = inbox.at[direction, phase + 1, b + 1]
        copies = []
        if b == 0:
            copies.append((has_low, remote(
                box, direction, phase + 1, rows + 1, side_sem.at[direction, phase, 0], pair, strip - 1)))
        if b == rows - 1:
            copies.append((has_high, remote(
                box, direction, phase + 1, 0, side_sem.at[direction, phase, 1], pair, strip + 1)))
        return copies

    def each(copies, what):
        for condition, copy in copies:
            if condition is None:
                what(copy)
            else:
                pl.when(condition)(functools.partial(what, copy))

    def start(copy):
        copy.start()

    def sent(copy):
        copy.wait_send()

    def arrived(direction, phase, slot):
        def wait():
            remote(
                inbox.at[direction, phase, slot], direction, phase, slot,
                next_sem.at[direction, 0], pair, strip,
            ).wait_recv()

        if slot == 0:
            pl.when(has_low)(wait)
        elif slot == rows + 1:
            pl.when(has_high)(wait)
        else:
            pl.when(phase == 0)(wait)

    def passed(direction, phase, b, value):
        inbox[direction, phase + 1, b + 1] = value.astype(jnp.bfloat16)
        each(sideways(direction, phase, b), start)

    def finish(step, direction, phase, par, b, moved, has_next):
        @pl.when(par == core)
        def _():
            source_here(down_source, direction, par, b).wait()

        @pl.when(par == other)
        def _():
            source_there(down_source, direction, par, b).wait_recv()

        value = source[direction, par, b]
        if moved is not None:
            value = value + moved
            accum[0, b] = value

            @pl.when((phase == PHASES - 1) & has_next)
            def _():
                outbox[direction, b] = accum[0, b].astype(jnp.bfloat16)
                each(onward(direction, b), start)

            @pl.when(phase < PHASES - 1)
            def _():
                passed(direction, phase, b, accum[0, b])

        else:
            passed(direction, phase, b, value)
        field[par, b] += value

        @pl.when((step == 1) & (par == other))
        def _():
            field_there(par, b).start()

        @pl.when((step == 1) & (par == core))
        def _():
            out_ref[:, columns(core, b)] = field[par, b]

    def one_phase(step, phase, direction, has_next):
        touched = set()
        done = 0
        half, odd = phase // 2, phase % 2
        par = jnp.where(direction == 0, half, 1 - half)
        for group in groups:
            for j in group:
                arrived(direction, phase, j)
                x = inbox[direction, phase, j]
                wide[:, pl.ds(j * depth, width)] = x
                wide[:, pl.ds(j * depth + width, width)] = jnp.concatenate([-x[cols:], x[:cols]], axis=0)
            for b in range(rows):
                taps = [j - b for j in group if 0 <= j - b <= 2]
                if not taps:
                    continue

                @pl.when((odd == 0) & (par == core))
                def _(b=b, taps=taps):
                    for k in taps:
                        tile_here(down_tiles, direction, par, b, k).wait()

                @pl.when((odd == 0) & (par == other))
                def _(b=b, taps=taps):
                    for k in taps:
                        tile_there(down_tiles, direction, par, b, k).wait_recv()

                runs = []
                for k in taps:
                    if runs and runs[-1][1] == k:
                        runs[-1][1] = k + 1
                    else:
                        runs.append([k, k + 1])
                total = None
                for low, high in runs:
                    part = jnp.dot(
                        wide[:, pl.ds((b + low) * depth, (high - low) * depth)],
                        weights[direction, par, b, pl.ds(low * depth, (high - low) * depth)],
                        preferred_element_type=jnp.float32,
                    )
                    total = part if total is None else total + part
                accum[odd, b] = accum[odd, b] + total if b in touched else total
                touched.add(b)
                done |= sum(1 << (3 * b + k) for k in taps)
                if (done >> (3 * b)) & 7 == 7:

                    @pl.when(odd == 0)
                    def _(b=b):
                        passed(direction, phase, b, accum[0, b])

                    @pl.when(odd == 1)
                    def _(b=b):
                        moved = jnp.where(thick[par] == 2, accum[1, b], accum[0, b])
                        finish(step, direction, phase, par, b, moved, has_next)

    def one_direction(step, carry):
        direction = (own_first + step) % 2
        begins = jnp.where(direction == 0, pair == 0, pair == pairs - 1)
        has_next = jnp.where(direction == 0, pair < pairs - 1, pair > 0)

        @pl.when(begins)
        def _():
            for b in edges_first:
                finish(step, direction, 1, direction, b, None, has_next)

        @pl.when(step == 0)
        def _():
            thick_there(other).wait_recv()

        def body(phase, inner):
            one_phase(step, phase, direction, has_next)
            return inner

        lax.fori_loop(jnp.where(begins, 2, 0), PHASES, body, 0)

        def drain(phase, inner):
            for b in range(rows):
                each(sideways(direction, phase, b), sent)
            return inner

        lax.fori_loop(jnp.where(begins, 1, 0), PHASES - 1, drain, 0)
        return carry

    lax.fori_loop(0, 2, one_direction, 0)

    for direction in range(2):
        for b in range(rows):
            source_there(source_refs[direction], direction, core, b).wait_send()
    thick_there(core).wait_send()
    tiles_in_order(lambda *at: tile_there(*at).wait_send())
    for direction in range(2):

        @pl.when(pair < pairs - 1 if direction == 0 else pair > 0)
        def _(direction=direction):
            for b in range(rows):
                each(onward(direction, b), sent)

    for b in range(rows):
        field_there(other, b).wait_recv()
        out_ref[:, columns(other, b)] = got[b]
    for b in range(rows):
        field_there(other, b).wait_send()


def shards(layers, tiles, down_tiles, up_tiles, down_source, up_source, thickness):
    _, blocks, taps, parts, width, _ = down_tiles.shape
    cols = down_source.shape[2]
    rows = blocks // 2
    height, depth = parts * cols, parts * width
    flat_tiles = (blocks, taps * depth, width)
    flat = (height, blocks * width)
    anywhere = pl.BlockSpec(memory_space=pl.ANY)
    dma = pltpu.SemaphoreType.DMA
    field = pl.pallas_call(
        functools.partial(sweep_kernel, layers, tiles, rows, width, cols),
        out_shape=jax.ShapeDtypeStruct(flat, jnp.float32),
        in_specs=[anywhere] * 4 + [pl.BlockSpec(memory_space=pltpu.SMEM)],
        out_specs=pl.BlockSpec(memory_space=pltpu.VMEM),
        scratch_shapes=[
            pltpu.VMEM((2, 2, rows, taps * depth, width), jnp.bfloat16),
            pltpu.VMEM((2, 2, rows, height, width), jnp.float32),
            pltpu.VMEM((2, PHASES, rows + 2, height, width), jnp.bfloat16),
            pltpu.VMEM((height, (rows + 2) * depth), jnp.bfloat16),
            pltpu.VMEM((2, rows, height, width), jnp.float32),
            pltpu.VMEM((2, rows, height, width), jnp.bfloat16),
            pltpu.VMEM((2, rows, height, width), jnp.float32),
            pltpu.VMEM((rows, height, width), jnp.float32),
            pltpu.VMEM((2, height, width), jnp.int32),
            dma((2, 2, rows, taps)),
            dma((2, rows, taps)),
            dma((2, 2, rows)),
            dma((2, rows)),
            dma((2, PHASES, rows + 2)),
            dma((2, rows)),
            dma((2, 2)),
            dma((2, PHASES - 1, 2)),
            dma((rows,)),
            dma((rows,)),
            dma,
            dma,
        ],
        compiler_params=pltpu.CompilerParams(
            collective_id=0, has_side_effects=True, vmem_limit_bytes=60 * 1024 * 1024
        ),
        cost_estimate=pl.CostEstimate(
            flops=16 * rows * taps * height * depth * width,
            bytes_accessed=8 * rows * taps * depth * width,
            transcendentals=0,
        ),
    )(
        down_tiles.reshape(flat_tiles),
        up_tiles.reshape(flat_tiles),
        down_source.reshape(flat),
        up_source.reshape(flat),
        thickness,
    )
    return field.reshape(down_source.shape)


def solution(mesh):
    return jax.shard_map(
        functools.partial(shards, mesh.shape["layer"], mesh.shape["tile"]),
        mesh=mesh,
        in_specs=(
            P("layer", "tile", None, None, None, None),
            P("layer", "tile", None, None, None, None),
            P("layer", None, None, "tile"),
            P("layer", None, None, "tile"),
            P("layer"),
        ),
        out_specs=P("layer", None, None, "tile"),
        check_vma=False,
    )
```

```python
import functools

import jax
import jax.numpy as jnp
from jax import lax
from jax.experimental import pallas as pl
from jax.experimental.pallas import tpu as pltpu
from jax.sharding import PartitionSpec as P

MESH = pl.DeviceIdType.MESH
PHASES = 4


def sweep_kernel(
    layers, tiles, rows, width, cols,
    down_tiles, up_tiles, down_source, up_source, thick_ref, out_ref,
    weights, source, inbox, wide, accum, outbox, field, got, thick,
    tile_sem, tile_sent, source_sem, source_sent, recv_sem, next_sem, rim_sem, side_sem,
    field_sem, field_sent, thick_sem, thick_sent,
):
    layer = lax.axis_index("layer")
    tile = lax.axis_index("tile")
    pairs, strips = layers // 2, tiles * 2
    pair, core = layer // 2, layer % 2
    other = 1 - core
    strip = tile * 2 + core
    height = 2 * cols
    depth = 2 * width
    has_low, has_high = strip > 0, strip < strips - 1
    own_first = jnp.where(2 * pair < pairs, 0, 1)

    products = 3 * rows

    def loop(low, high, what):
        def body(index, carry):
            what(index)
            return carry

        lax.fori_loop(low, high, body, 0)

    def device(to_pair, to_strip):
        return {"layer": 2 * to_pair + to_strip % 2, "tile": to_strip // 2}

    partner = {"layer": 2 * pair + other, "tile": tile}

    def columns(part, b):
        return pl.ds(pl.multiple_of((part * rows + b) * width, width), width)

    def tile_here(ref, direction, par, b, k):
        taps = pl.ds(pl.multiple_of(k * depth, depth), depth)
        return pltpu.make_async_copy(
            ref.at[core * rows + b, taps], weights.at[direction, par, b, taps],
            tile_sem.at[direction, par, b, k],
        )

    def tile_there(ref, direction, par, b, k):
        taps = pl.ds(pl.multiple_of(k * depth, depth), depth)
        return pltpu.make_async_remote_copy(
            src_ref=ref.at[other * rows + b, taps], dst_ref=weights.at[direction, par, b, taps],
            send_sem=tile_sent.at[direction, b, k], recv_sem=tile_sem.at[direction, par, b, k],
            device_id=partner, device_id_type=MESH,
        )

    def source_here(ref, direction, par, b):
        return pltpu.make_async_copy(
            ref.at[:, columns(core, b)], source.at[direction, par, b], source_sem.at[direction, par, b]
        )

    def source_there(ref, direction, par, b):
        return pltpu.make_async_remote_copy(
            src_ref=ref.at[:, columns(other, b)], dst_ref=source.at[direction, par, b],
            send_sem=source_sent.at[direction, b], recv_sem=source_sem.at[direction, par, b],
            device_id=partner, device_id_type=MESH,
        )

    def thick_there(par):
        return pltpu.make_async_remote_copy(
            src_ref=thick.at[par], dst_ref=thick.at[par], send_sem=thick_sent, recv_sem=thick_sem,
            device_id=partner, device_id_type=MESH,
        )

    def field_there(par, b):
        return pltpu.make_async_remote_copy(
            src_ref=field.at[par, b], dst_ref=got.at[b], send_sem=field_sent.at[b],
            recv_sem=field_sem.at[b], device_id=partner, device_id_type=MESH,
        )

    refs = ((down_tiles, down_source), (up_tiles, up_source))
    used = (layer > 0, layer < layers - 1)

    def each_direction(what):
        def one(step):
            chosen = (own_first + step) % 2
            for direction in range(2):
                pl.when(chosen == direction)(functools.partial(what, direction))

        loop(0, 2, one)

    def loads(direction, of_tile, of_source):
        tiles_ref, source_ref = refs[direction]
        loop(0, rows, lambda b: of_source(source_ref, direction, core, b))

        @pl.when(used[direction])
        def _():
            loop(1, products - 1, lambda i: of_tile(tiles_ref, direction, core, i // 3, i % 3))
            for i in (0, products - 1):
                of_tile(tiles_ref, direction, core, i // 3, i % 3)

    each_direction(lambda direction: loads(
        direction, lambda *at: tile_here(*at).start(), lambda *at: source_here(*at).start()))

    barrier = pltpu.get_barrier_semaphore()
    met = 0
    for dp in (-1, 0, 1):
        for ds in (-1, 0, 1):
            if dp == 0 and ds == 0:
                continue
            there = (pair + dp >= 0) & (pair + dp < pairs) & (strip + ds >= 0) & (strip + ds < strips)

            @pl.when(there)
            def _(dp=dp, ds=ds):
                pl.semaphore_signal(
                    barrier, inc=1, device_id=device(pair + dp, strip + ds), device_id_type=MESH
                )

            met = met + jnp.where(there, 1, 0)

    field[...] = jnp.zeros_like(field)
    thick[core] = jnp.full((height, width), thick_ref[0], jnp.int32)
    no_trace = jnp.zeros((height, width), jnp.bfloat16)
    for absent, slot in ((jnp.logical_not(has_low), 0), (jnp.logical_not(has_high), rows + 1)):

        @pl.when(absent)
        def _(slot=slot):
            for direction in range(2):
                for phase in range(PHASES):
                    inbox[direction, phase, slot] = no_trace

    pl.semaphore_wait(barrier, met)
    thick_there(core).start()
    each_direction(lambda direction: loads(
        direction, lambda *at: tile_there(*at).start(), lambda *at: source_there(*at).start()))

    def remote(src, direction, phase, slot, send_sem, to_pair, to_strip):
        return pltpu.make_async_remote_copy(
            src_ref=src, dst_ref=inbox.at[direction, phase, slot], send_sem=send_sem,
            recv_sem=recv_sem.at[direction, phase, slot],
            device_id=device(to_pair, to_strip), device_id_type=MESH,
        )

    def onward(direction, b):
        return remote(
            outbox.at[direction, b], direction, 0, b + 1, next_sem.at[direction, b],
            pair + 1 - 2 * direction, strip)

    def rim(direction, side):
        return remote(
            outbox.at[direction, side * (rows - 1)], direction, 0, (1 - side) * (rows + 1),
            rim_sem.at[direction, side], pair + 1 - 2 * direction, strip + 2 * side - 1)

    def sideways(direction, phase, side):
        return remote(
            inbox.at[direction, phase + 1, 1 + side * (rows - 1)], direction, phase + 1,
            (1 - side) * (rows + 1), side_sem.at[direction, phase, side], pair, strip + 2 * side - 1)

    def has(side):
        return jnp.where(side == 0, has_low, has_high)

    def arrived(direction, phase, slot):
        remote(
            inbox.at[direction, phase, slot], direction, phase, slot,
            next_sem.at[direction, 0], pair, strip,
        ).wait_recv()

    def passed(direction, phase, b, sides):
        inbox[direction, phase + 1, b + 1] = accum[0, b].astype(jnp.bfloat16)
        for side in sides:
            pl.when(has(side))(lambda side=side: sideways(direction, phase, side).start())

    def finish(step, direction, phase, par, b, moved, sides, has_next):
        @pl.when(par == core)
        def _():
            source_here(down_source, direction, par, b).wait()

        @pl.when(par == other)
        def _():
            source_there(down_source, direction, par, b).wait_recv()

        value = source[direction, par, b] + moved if moved is not None else source[direction, par, b]
        accum[0, b] = value

        @pl.when((phase == PHASES - 1) & has_next)
        def _():
            outbox[direction, b] = accum[0, b].astype(jnp.bfloat16)
            for side in sides:
                pl.when(has(side))(lambda side=side: rim(direction, side).start())
            onward(direction, b).start()

        @pl.when(phase < PHASES - 1)
        def _():
            passed(direction, phase, b, sides)

        field[par, b] += accum[0, b]

        @pl.when((step == 1) & (par == other))
        def _():
            field_there(par, b).start()

        @pl.when((step == 1) & (par == core))
        def _():
            out_ref[:, columns(core, b)] = field[par, b]

    def widen(direction, phase, slot):
        x = inbox[direction, phase, slot]
        wide[slot, :, pl.ds(0, width)] = x
        wide[slot, :, pl.ds(width, width)] = jnp.concatenate([-x[cols:], x[:cols]], axis=0)

    def product(direction, par, odd, b, k):
        @pl.when((odd == 0) & (par == core))
        def _():
            tile_here(down_tiles, direction, par, b, k).wait()

        @pl.when((odd == 0) & (par == other))
        def _():
            tile_there(down_tiles, direction, par, b, k).wait_recv()

        accum[odd, b] += jnp.dot(
            wide[b + k], weights[direction, par, b, pl.ds(pl.multiple_of(k * depth, depth), depth)],
            preferred_element_type=jnp.float32,
        )

    def one_phase(step, phase, direction, has_next):
        half, odd = phase // 2, phase % 2
        par = jnp.where(direction == 0, half, 1 - half)

        def own_input(b):
            pl.when(phase == 0)(lambda: arrived(direction, phase, b + 1))
            widen(direction, phase, b + 1)
            accum[odd, b] = jnp.zeros((height, width), jnp.float32)

        loop(0, rows, own_input)
        loop(1, products - 1, lambda i: product(direction, par, odd, i // 3, i % 3))

        def complete(b, sides):
            @pl.when(odd == 0)
            def _():
                passed(direction, phase, b, sides)

            @pl.when(odd == 1)
            def _():
                moved = jnp.where(thick[par] == 2, accum[1, b], accum[0, b])
                finish(step, direction, phase, par, b, moved, sides, has_next)

        def rim_input(index):
            side = (1 - core + index) % 2
            slot, b = side * (rows + 1), side * (rows - 1)
            pl.when(has(side))(lambda: arrived(direction, phase, slot))
            widen(direction, phase, slot)
            product(direction, par, odd, b, 2 * side)
            if rows > 1:
                complete(b, [side])

        loop(0, 2, rim_input)
        if rows == 1:
            complete(0, [0, 1])
        elif rows > 2:
            loop(1, rows - 1, lambda b: complete(b, []))

    def one_direction(step, carry):
        direction = (own_first + step) % 2
        begins = jnp.where(direction == 0, pair == 0, pair == pairs - 1)
        has_next = jnp.where(direction == 0, pair < pairs - 1, pair > 0)

        @pl.when(begins)
        def _():
            for b in range(rows):
                sides = [side for side in range(2) if b == side * (rows - 1)]
                finish(step, direction, 1, direction, b, None, sides, has_next)

        @pl.when(step == 0)
        def _():
            thick_there(other).wait_recv()

        def body(phase, inner):
            one_phase(step, phase, direction, has_next)
            return inner

        lax.fori_loop(jnp.where(begins, 2, 0), PHASES, body, 0)

        def drain(phase, inner):
            for side in range(2):
                pl.when(has(side))(lambda side=side: sideways(direction, phase, side).wait_send())
            return inner

        lax.fori_loop(jnp.where(begins, 1, 0), PHASES - 1, drain, 0)

        @pl.when(has_next)
        def _():
            loop(0, rows, lambda b: onward(direction, b).wait_send())
            for side in range(2):
                pl.when(has(side))(lambda side=side: rim(direction, side).wait_send())

        return carry

    lax.fori_loop(0, 2, one_direction, 0)

    thick_there(core).wait_send()
    each_direction(lambda direction: loads(
        direction, lambda *at: tile_there(*at).wait_send(), lambda *at: source_there(*at).wait_send()))

    for b in range(rows):
        field_there(other, b).wait_recv()
        out_ref[:, columns(other, b)] = got[b]
    for b in range(rows):
        field_there(other, b).wait_send()


def shards(layers, tiles, down_tiles, up_tiles, down_source, up_source, thickness):
    _, blocks, taps, parts, width, _ = down_tiles.shape
    cols = down_source.shape[2]
    rows = blocks // 2
    height, depth = parts * cols, parts * width
    flat_tiles = (blocks, taps * depth, width)
    flat = (height, blocks * width)
    anywhere = pl.BlockSpec(memory_space=pl.ANY)
    dma = pltpu.SemaphoreType.DMA
    field = pl.pallas_call(
        functools.partial(sweep_kernel, layers, tiles, rows, width, cols),
        out_shape=jax.ShapeDtypeStruct(flat, jnp.float32),
        in_specs=[anywhere] * 4 + [pl.BlockSpec(memory_space=pltpu.SMEM)],
        out_specs=pl.BlockSpec(memory_space=pltpu.VMEM),
        scratch_shapes=[
            pltpu.VMEM((2, 2, rows, taps * depth, width), jnp.bfloat16),
            pltpu.VMEM((2, 2, rows, height, width), jnp.float32),
            pltpu.VMEM((2, PHASES, rows + 2, height, width), jnp.bfloat16),
            pltpu.VMEM((rows + 2, height, depth), jnp.bfloat16),
            pltpu.VMEM((2, rows, height, width), jnp.float32),
            pltpu.VMEM((2, rows, height, width), jnp.bfloat16),
            pltpu.VMEM((2, rows, height, width), jnp.float32),
            pltpu.VMEM((rows, height, width), jnp.float32),
            pltpu.VMEM((2, height, width), jnp.int32),
            dma((2, 2, rows, taps)),
            dma((2, rows, taps)),
            dma((2, 2, rows)),
            dma((2, rows)),
            dma((2, PHASES, rows + 2)),
            dma((2, rows)),
            dma((2, 2)),
            dma((2, PHASES - 1, 2)),
            dma((rows,)),
            dma((rows,)),
            dma,
            dma,
        ],
        compiler_params=pltpu.CompilerParams(
            collective_id=0, has_side_effects=True, vmem_limit_bytes=60 * 1024 * 1024
        ),
        cost_estimate=pl.CostEstimate(
            flops=16 * rows * taps * height * depth * width,
            bytes_accessed=8 * rows * taps * depth * width,
            transcendentals=0,
        ),
    )(
        down_tiles.reshape(flat_tiles),
        up_tiles.reshape(flat_tiles),
        down_source.reshape(flat),
        up_source.reshape(flat),
        thickness,
    )
    return field.reshape(down_source.shape)


def solution(mesh):
    return jax.shard_map(
        functools.partial(shards, mesh.shape["layer"], mesh.shape["tile"]),
        mesh=mesh,
        in_specs=(
            P("layer", "tile", None, None, None, None),
            P("layer", "tile", None, None, None, None),
            P("layer", None, None, "tile"),
            P("layer", None, None, "tile"),
            P("layer"),
        ),
        out_specs=P("layer", None, None, "tile"),
        check_vma=False,
    )
```

```python
import functools

import jax
import jax.numpy as jnp
from jax import lax
from jax.experimental import pallas as pl
from jax.experimental.pallas import tpu as pltpu
from jax.sharding import PartitionSpec as P

MESH = pl.DeviceIdType.MESH


def sweep_kernel(
    layers, tiles, rows, width, cols,
    down_tiles, up_tiles, down_source, up_source, thick_ref, out_ref,
    weights, source, inbox, wide, accum, first, outbox,
    tile_sem, source_sem, recv_sem, next_sem, rim_sem, mid_sem,
):
    layer = lax.axis_index("layer")
    tile = lax.axis_index("tile")
    height = 2 * cols
    depth = 2 * width
    slots = rows + 2
    has_low, has_high = tile > 0, tile < tiles - 1
    own_first = jnp.where(2 * layer < layers, 0, 1)

    groups = [g for g in (list(range(2, rows)), sorted({1, rows}), [0], [rows + 1]) if g]

    def tile_copy(ref, direction, b, k):
        return pltpu.make_async_copy(
            ref.at[b, pl.ds(k * depth, depth)],
            weights.at[direction, b, pl.ds(k * depth, depth)],
            tile_sem.at[direction, b, k],
        )

    def source_copy(ref, direction, b):
        return pltpu.make_async_copy(
            ref.at[:, pl.ds(b * width, width)], source.at[direction, b], source_sem.at[direction, b]
        )

    tile_order = [(b, j - b) for g in groups for j in g for b in range(rows) if 0 <= j - b <= 2]

    def start_loads(ref, direction):
        for b, k in tile_order:
            tile_copy(ref, direction, b, k).start()

    for direction, ref in enumerate((down_source, up_source)):
        for b in range(rows):
            source_copy(ref, direction, b).start()

    @pl.when(own_first == 0)
    def _():
        start_loads(down_tiles, 0)
        start_loads(up_tiles, 1)

    @pl.when(own_first == 1)
    def _():
        start_loads(up_tiles, 1)
        start_loads(down_tiles, 0)

    barrier = pltpu.get_barrier_semaphore()
    met = 0
    for dl in (-1, 0, 1):
        for dt in (-1, 0, 1):
            if dl == 0 and dt == 0:
                continue
            there = (layer + dl >= 0) & (layer + dl < layers) & (tile + dt >= 0) & (tile + dt < tiles)

            @pl.when(there)
            def _(dl=dl, dt=dt):
                pl.semaphore_signal(
                    barrier, inc=1, device_id={"layer": layer + dl, "tile": tile + dt}, device_id_type=MESH
                )

            met = met + jnp.where(there, 1, 0)

    out_ref[...] = jnp.zeros_like(out_ref)
    no_trace = jnp.zeros((height, width), jnp.bfloat16)

    @pl.when(jnp.logical_not(has_low))
    def _():
        for direction in range(2):
            for phase in range(2):
                inbox[direction, phase, 0] = no_trace

    @pl.when(jnp.logical_not(has_high))
    def _():
        for direction in range(2):
            for phase in range(2):
                inbox[direction, phase, rows + 1] = no_trace

    pl.semaphore_wait(barrier, met)
    is_thick = jnp.full((height, width), thick_ref[0], jnp.int32) == 2

    pieces = height // 16 if height % 16 == 0 else 1

    def remote(src, direction, phase, slot, send_sem, to_layer, to_tile, piece=None):
        dst = inbox.at[direction, phase, slot]
        if piece is not None:
            span = pl.ds(piece * (height // pieces), height // pieces)
            src, dst = src.at[span], dst.at[span]
        return pltpu.make_async_remote_copy(
            src_ref=src,
            dst_ref=dst,
            send_sem=send_sem,
            recv_sem=recv_sem.at[direction, phase, slot],
            device_id={"layer": to_layer, "tile": to_tile},
            device_id_type=MESH,
        )

    def onward(direction, b):
        to_layer = layer + 1 - 2 * direction
        box = outbox.at[direction, b]
        copies = []
        if b == 0:
            copies.append((has_low, functools.partial(
                remote, box, direction, 0, rows + 1, rim_sem.at[direction, 0], to_layer, tile - 1)))
        if b == rows - 1:
            copies.append((has_high, functools.partial(
                remote, box, direction, 0, 0, rim_sem.at[direction, 1], to_layer, tile + 1)))
        copies.append((None, functools.partial(
            remote, box, direction, 0, b + 1, next_sem.at[direction, b], to_layer, tile)))
        return copies

    def sideways(direction, b):
        box = inbox.at[direction, 1, b + 1]
        copies = []
        if b == 0:
            copies.append((has_low, functools.partial(
                remote, box, direction, 1, rows + 1, mid_sem.at[direction, 0], layer, tile - 1)))
        if b == rows - 1:
            copies.append((has_high, functools.partial(
                remote, box, direction, 1, 0, mid_sem.at[direction, 1], layer, tile + 1)))
        return copies

    def each(copies, what):
        for condition, copy in copies:
            if condition is None:
                what(copy)
            else:
                pl.when(condition)(functools.partial(what, copy))

    def start(copy):
        for piece in range(pieces):
            copy(piece=piece).start()

    def sent(copy):
        copy().wait_send()

    def arrived(direction, phase, slot):
        def wait():
            remote(
                inbox.at[direction, phase, slot], direction, phase, slot,
                mid_sem.at[direction, 0], layer, tile,
            ).wait_recv()

        if slot == 0:
            pl.when(has_low)(wait)
        elif slot == rows + 1:
            pl.when(has_high)(wait)
        else:
            pl.when(phase == 0)(wait)

    def finish(direction, b, moved, has_next):
        columns = pl.ds(b * width, width)
        source_copy(down_source, direction, b).wait()
        value = source[direction, b]
        if moved is not None:
            value = value + moved

        @pl.when(has_next)
        def _():
            outbox[direction, b] = value.astype(jnp.bfloat16)
            each(onward(direction, b), start)

        out_ref[:, columns] += value

    def one_phase(phase, direction, has_next):
        touched = set()
        done = 0
        for group in groups:
            for j in group:
                arrived(direction, phase, j)
                x = inbox[direction, phase, j]
                wide[:, pl.ds(j * depth, width)] = x
                wide[:, pl.ds(j * depth + width, width)] = jnp.concatenate([-x[cols:], x[:cols]], axis=0)
            outs = [b for b in range(rows) if any(0 <= j - b <= 2 for j in group)]
            ready = []
            for b in outs:
                taps = [j - b for j in group if 0 <= j - b <= 2]

                @pl.when(phase == 0)
                def _(b=b, taps=taps):
                    for k in taps:
                        tile_copy(down_tiles, direction, b, k).wait()

                runs = []
                for k in taps:
                    if runs and runs[-1][1] == k:
                        runs[-1][1] = k + 1
                    else:
                        runs.append([k, k + 1])
                total = None
                for low, high in runs:
                    part = jnp.dot(
                        wide[:, pl.ds((b + low) * depth, (high - low) * depth)],
                        weights[direction, b, pl.ds(low * depth, (high - low) * depth)],
                        preferred_element_type=jnp.float32,
                    )
                    total = part if total is None else total + part
                accum[b] = accum[b] + total if b in touched else total
                touched.add(b)
                done |= sum(1 << (3 * b + k) for k in taps)
                if (done >> (3 * b)) & 7 == 7:
                    ready.append(b)

                    @pl.when(phase == 0)
                    def _(b=b):
                        inbox[direction, 1, b + 1] = accum[b].astype(jnp.bfloat16)
                        each(sideways(direction, b), start)
                        first[b] = accum[b]

                    @pl.when(phase == 1)
                    def _(b=b):
                        finish(direction, b, jnp.where(is_thick, accum[b], first[b]), has_next)

    def one_direction(step, carry):
        direction = (own_first + step) % 2
        begins = jnp.where(direction == 0, layer == 0, layer == layers - 1)
        has_next = jnp.where(direction == 0, layer < layers - 1, layer > 0)

        @pl.when(begins)
        def _():
            for b in sorted(range(rows), key=lambda b: 0 < b < rows - 1):
                finish(direction, b, None, has_next)
            for b, k in tile_order:
                tile_copy(down_tiles, direction, b, k).wait()

        @pl.when(jnp.logical_not(begins))
        def _():
            def body(phase, inner):
                one_phase(phase, direction, has_next)
                return inner

            lax.fori_loop(0, 2, body, 0)
            for b in range(rows):
                each(sideways(direction, b), sent)

        return carry

    lax.fori_loop(0, 2, one_direction, 0)
    for direction in range(2):
        has_next = layer < layers - 1 if direction == 0 else layer > 0

        @pl.when(has_next)
        def _(direction=direction):
            for b in range(rows):
                each(onward(direction, b), sent)


def shards(layers, tiles, down_tiles, up_tiles, down_source, up_source, thickness):
    _, rows, taps, parts, width, _ = down_tiles.shape
    cols = down_source.shape[2]
    height, depth = parts * cols, parts * width
    points = rows * width
    flat_tiles = (rows, taps * depth, width)
    flat = (height, points)
    anywhere = pl.BlockSpec(memory_space=pl.ANY)
    field = pl.pallas_call(
        functools.partial(sweep_kernel, layers, tiles, rows, width, cols),
        out_shape=jax.ShapeDtypeStruct(flat, jnp.float32),
        in_specs=[anywhere] * 4 + [pl.BlockSpec(memory_space=pltpu.SMEM)],
        out_specs=pl.BlockSpec(memory_space=pltpu.VMEM),
        scratch_shapes=[
            pltpu.VMEM((2,) + flat_tiles, jnp.bfloat16),
            pltpu.VMEM((2, rows, height, width), jnp.float32),
            pltpu.VMEM((2, 2, rows + 2, height, width), jnp.bfloat16),
            pltpu.VMEM((height, (rows + 2) * depth), jnp.bfloat16),
            pltpu.VMEM((rows, height, width), jnp.float32),
            pltpu.VMEM((rows, height, width), jnp.float32),
            pltpu.VMEM((2, rows, height, width), jnp.bfloat16),
            pltpu.SemaphoreType.DMA((2, rows, taps)),
            pltpu.SemaphoreType.DMA((2, rows)),
            pltpu.SemaphoreType.DMA((2, 2, rows + 2)),
            pltpu.SemaphoreType.DMA((2, rows)),
            pltpu.SemaphoreType.DMA((2, 2)),
            pltpu.SemaphoreType.DMA((2, 2)),
        ],
        compiler_params=pltpu.CompilerParams(
            collective_id=0, has_side_effects=True, vmem_limit_bytes=48 * 1024 * 1024
        ),
        cost_estimate=pl.CostEstimate(
            flops=8 * rows * taps * height * depth * width,
            bytes_accessed=4 * rows * taps * depth * width,
            transcendentals=0,
        ),
    )(
        down_tiles.reshape(flat_tiles),
        up_tiles.reshape(flat_tiles),
        down_source.reshape(flat),
        up_source.reshape(flat),
        thickness,
    )
    return field.reshape(down_source.shape)


def solution(mesh):
    return jax.shard_map(
        functools.partial(shards, mesh.shape["layer"], mesh.shape["tile"]),
        mesh=mesh,
        in_specs=(
            P("layer", "tile", None, None, None, None),
            P("layer", "tile", None, None, None, None),
            P("layer", None, None, "tile"),
            P("layer", None, None, "tile"),
            P("layer"),
        ),
        out_specs=P("layer", None, None, "tile"),
        check_vma=False,
    )
```

```python
import functools

import jax
import jax.numpy as jnp
from jax import lax
from jax.experimental import pallas as pl
from jax.experimental.pallas import tpu as pltpu
from jax.sharding import PartitionSpec as P

MESH = pl.DeviceIdType.MESH


def sweep_kernel(
    layers, tiles, rows, width, cols,
    down_tiles, up_tiles, down_source, up_source, thick_ref, out_ref,
    weights, source, inbox, wide, accum, first, outbox,
    tile_sem, source_sem, recv_sem, next_sem, rim_sem, mid_sem,
):
    layer = lax.axis_index("layer")
    tile = lax.axis_index("tile")
    height = 2 * cols
    depth = 2 * width
    slots = rows + 2
    has_low, has_high = tile > 0, tile < tiles - 1
    own_first = jnp.where(2 * layer < layers, 0, 1)

    groups = [g for g in (list(range(2, rows)), sorted({1, rows}), [0], [rows + 1]) if g]

    def tile_copy(ref, direction, b, k):
        return pltpu.make_async_copy(
            ref.at[b, pl.ds(k * depth, depth)],
            weights.at[direction, b, pl.ds(k * depth, depth)],
            tile_sem.at[direction, b, k],
        )

    def source_copy(ref, direction, b):
        return pltpu.make_async_copy(
            ref.at[:, pl.ds(b * width, width)], source.at[direction, b], source_sem.at[direction, b]
        )

    tile_order = [(b, j - b) for g in groups for j in g for b in range(rows) if 0 <= j - b <= 2]

    def start_loads(ref, direction):
        for b, k in tile_order:
            tile_copy(ref, direction, b, k).start()

    for direction, ref in enumerate((down_source, up_source)):
        for b in range(rows):
            source_copy(ref, direction, b).start()

    @pl.when(own_first == 0)
    def _():
        start_loads(down_tiles, 0)
        start_loads(up_tiles, 1)

    @pl.when(own_first == 1)
    def _():
        start_loads(up_tiles, 1)
        start_loads(down_tiles, 0)

    barrier = pltpu.get_barrier_semaphore()
    met = 0
    for dl in (-1, 0, 1):
        for dt in (-1, 0, 1):
            if dl == 0 and dt == 0:
                continue
            there = (layer + dl >= 0) & (layer + dl < layers) & (tile + dt >= 0) & (tile + dt < tiles)

            @pl.when(there)
            def _(dl=dl, dt=dt):
                pl.semaphore_signal(
                    barrier, inc=1, device_id={"layer": layer + dl, "tile": tile + dt}, device_id_type=MESH
                )

            met = met + jnp.where(there, 1, 0)

    out_ref[...] = jnp.zeros_like(out_ref)
    no_trace = jnp.zeros((height, width), jnp.bfloat16)

    @pl.when(jnp.logical_not(has_low))
    def _():
        for direction in range(2):
            for phase in range(2):
                inbox[direction, phase, 0] = no_trace

    @pl.when(jnp.logical_not(has_high))
    def _():
        for direction in range(2):
            for phase in range(2):
                inbox[direction, phase, rows + 1] = no_trace

    pl.semaphore_wait(barrier, met)
    is_thick = jnp.full((height, width), thick_ref[0], jnp.int32) == 2

    pieces = height // 16 if height % 16 == 0 else 1

    def remote(src, direction, phase, slot, send_sem, to_layer, to_tile, piece=None):
        dst = inbox.at[direction, phase, slot]
        if piece is not None:
            span = pl.ds(piece * (height // pieces), height // pieces)
            src, dst = src.at[span], dst.at[span]
        return pltpu.make_async_remote_copy(
            src_ref=src,
            dst_ref=dst,
            send_sem=send_sem,
            recv_sem=recv_sem.at[direction, phase, slot],
            device_id={"layer": to_layer, "tile": to_tile},
            device_id_type=MESH,
        )

    def onward(direction, b):
        to_layer = layer + 1 - 2 * direction
        box = outbox.at[direction, b]
        copies = []
        if b == 0:
            copies.append((has_low, functools.partial(
                remote, box, direction, 0, rows + 1, rim_sem.at[direction, 0], to_layer, tile - 1)))
        if b == rows - 1:
            copies.append((has_high, functools.partial(
                remote, box, direction, 0, 0, rim_sem.at[direction, 1], to_layer, tile + 1)))
        copies.append((None, functools.partial(
            remote, box, direction, 0, b + 1, next_sem.at[direction, b], to_layer, tile)))
        return copies

    def sideways(direction, b):
        box = inbox.at[direction, 1, b + 1]
        copies = []
        if b == 0:
            copies.append((has_low, functools.partial(
                remote, box, direction, 1, rows + 1, mid_sem.at[direction, 0], layer, tile - 1)))
        if b == rows - 1:
            copies.append((has_high, functools.partial(
                remote, box, direction, 1, 0, mid_sem.at[direction, 1], layer, tile + 1)))
        return copies

    def each(copies, what):
        for condition, copy in copies:
            if condition is None:
                what(copy)
            else:
                pl.when(condition)(functools.partial(what, copy))

    def start(copy):
        for piece in range(pieces):
            copy(piece=piece).start()

    def sent(copy):
        copy().wait_send()

    def arrived(direction, phase, slot):
        def wait():
            remote(
                inbox.at[direction, phase, slot], direction, phase, slot,
                mid_sem.at[direction, 0], layer, tile,
            ).wait_recv()

        if slot == 0:
            pl.when(has_low)(wait)
        elif slot == rows + 1:
            pl.when(has_high)(wait)
        else:
            pl.when(phase == 0)(wait)

    def finish(direction, b, moved, has_next):
        columns = pl.ds(b * width, width)
        source_copy(down_source, direction, b).wait()
        value = source[direction, b]
        if moved is not None:
            value = value + moved

        @pl.when(has_next)
        def _():
            outbox[direction, b] = value.astype(jnp.bfloat16)
            each(onward(direction, b), start)

        out_ref[:, columns] += value

    def one_phase(phase, direction, has_next):
        touched = set()
        done = 0
        for group in groups:
            for j in group:
                arrived(direction, phase, j)
                x = inbox[direction, phase, j]
                wide[:, pl.ds(j * depth, width)] = x
                wide[:, pl.ds(j * depth + width, width)] = jnp.concatenate([-x[cols:], x[:cols]], axis=0)
            outs = [b for b in range(rows) if any(0 <= j - b <= 2 for j in group)]
            ready = []
            for b in outs:
                taps = [j - b for j in group if 0 <= j - b <= 2]

                @pl.when(phase == 0)
                def _(b=b, taps=taps):
                    for k in taps:
                        tile_copy(down_tiles, direction, b, k).wait()

                runs = []
                for k in taps:
                    if runs and runs[-1][1] == k:
                        runs[-1][1] = k + 1
                    else:
                        runs.append([k, k + 1])
                total = None
                for low, high in runs:
                    part = jnp.dot(
                        wide[:, pl.ds((b + low) * depth, (high - low) * depth)],
                        weights[direction, b, pl.ds(low * depth, (high - low) * depth)],
                        preferred_element_type=jnp.float32,
                    )
                    total = part if total is None else total + part
                accum[b] = accum[b] + total if b in touched else total
                touched.add(b)
                done |= sum(1 << (3 * b + k) for k in taps)
                if (done >> (3 * b)) & 7 == 7:
                    ready.append(b)

                    @pl.when(phase == 0)
                    def _(b=b):
                        inbox[direction, 1, b + 1] = accum[b].astype(jnp.bfloat16)
                        each(sideways(direction, b), start)
                        first[b] = accum[b]

                    @pl.when(phase == 1)
                    def _(b=b):
                        finish(direction, b, jnp.where(is_thick, accum[b], first[b]), has_next)

    def one_direction(step, carry):
        direction = (own_first + step) % 2
        begins = jnp.where(direction == 0, layer == 0, layer == layers - 1)
        has_next = jnp.where(direction == 0, layer < layers - 1, layer > 0)

        @pl.when(begins)
        def _():
            for b in sorted(range(rows), key=lambda b: 0 < b < rows - 1):
                finish(direction, b, None, has_next)
            for b, k in tile_order:
                tile_copy(down_tiles, direction, b, k).wait()

        @pl.when(jnp.logical_not(begins))
        def _():
            def body(phase, inner):
                one_phase(phase, direction, has_next)
                return inner

            lax.fori_loop(0, 2, body, 0)
            for b in range(rows):
                each(sideways(direction, b), sent)

        return carry

    lax.fori_loop(0, 2, one_direction, 0)
    for direction in range(2):
        has_next = layer < layers - 1 if direction == 0 else layer > 0

        @pl.when(has_next)
        def _(direction=direction):
            for b in range(rows):
                each(onward(direction, b), sent)


def shards(layers, tiles, down_tiles, up_tiles, down_source, up_source, thickness):
    _, rows, taps, parts, width, _ = down_tiles.shape
    cols = down_source.shape[2]
    height, depth = parts * cols, parts * width
    points = rows * width
    flat_tiles = (rows, taps * depth, width)
    flat = (height, points)
    anywhere = pl.BlockSpec(memory_space=pl.ANY)
    field = pl.pallas_call(
        functools.partial(sweep_kernel, layers, tiles, rows, width, cols),
        out_shape=jax.ShapeDtypeStruct(flat, jnp.float32),
        in_specs=[anywhere] * 4 + [pl.BlockSpec(memory_space=pltpu.SMEM)],
        out_specs=pl.BlockSpec(memory_space=pltpu.VMEM),
        scratch_shapes=[
            pltpu.VMEM((2,) + flat_tiles, jnp.bfloat16),
            pltpu.VMEM((2, rows, height, width), jnp.float32),
            pltpu.VMEM((2, 2, rows + 2, height, width), jnp.bfloat16),
            pltpu.VMEM((height, (rows + 2) * depth), jnp.bfloat16),
            pltpu.VMEM((rows, height, width), jnp.float32),
            pltpu.VMEM((rows, height, width), jnp.float32),
            pltpu.VMEM((2, rows, height, width), jnp.bfloat16),
            pltpu.SemaphoreType.DMA((2, rows, taps)),
            pltpu.SemaphoreType.DMA((2, rows)),
            pltpu.SemaphoreType.DMA((2, 2, rows + 2)),
            pltpu.SemaphoreType.DMA((2, rows)),
            pltpu.SemaphoreType.DMA((2, 2)),
            pltpu.SemaphoreType.DMA((2, 2)),
        ],
        compiler_params=pltpu.CompilerParams(
            collective_id=0, has_side_effects=True, vmem_limit_bytes=60 * 1024 * 1024
        ),
        cost_estimate=pl.CostEstimate(
            flops=8 * rows * taps * height * depth * width,
            bytes_accessed=4 * rows * taps * depth * width,
            transcendentals=0,
        ),
    )(
        down_tiles.reshape(flat_tiles),
        up_tiles.reshape(flat_tiles),
        down_source.reshape(flat),
        up_source.reshape(flat),
        thickness,
    )
    return field.reshape(down_source.shape)


def solution(mesh):
    return jax.shard_map(
        functools.partial(shards, mesh.shape["layer"], mesh.shape["tile"]),
        mesh=mesh,
        in_specs=(
            P("layer", "tile", None, None, None, None),
            P("layer", "tile", None, None, None, None),
            P("layer", None, None, "tile"),
            P("layer", None, None, "tile"),
            P("layer"),
        ),
        out_specs=P("layer", None, None, "tile"),
        check_vma=False,
    )
```
